256 devices in a mesh: chan: 8 (over y, core), seq: 32 (over z, x).
Axes of the slice: x: 4, y: 4, z: 8, core: 2. Of those that a mesh axis runs over, the one named last changes fastest.
Arguments:
- projected: bfloat16 [8192, 3, 4096], P('seq', None, 'chan'), may hold values from -6 to 6
- short_taps: float32 [7, 3, 4096], P(None, None, 'chan'), may hold values from -2.5 to 2.5
- long_filter: bfloat16 [8192, 4096], P('seq', 'chan'), may hold values from -0.0625 to 0.0625
- skip_gain: float32 [4096], P('chan'), may hold values from 0.5 to 1.5
- out_weight: bfloat16 [4096, 4096], P('chan'), may hold values from -0.125 to 0.125
Outputs:
- mixed: bfloat16 [4096, 8192], P('chan', 'seq')
The draws below stay inside these ranges and needn't reach their ends.
All inputs are finite; a program needn't handle non-finite values.
Results may differ from the reference program's by a relative error of at most 0.014.
Values may be sent and summed in bfloat16 or wider, within the bound.
A program may use at most 64 MiB of HBM per device.

```python
import jax
import jax.numpy as jnp
from jax import lax

C = 4096
TAPS = 7
L = 8192


def strengthened(drawn, key, source, target, shards_of, factor):
    owner, partner = [(jnp.arange(drawn.shape[axis_at]) // (drawn.shape[axis_at] // shards_of)).reshape([-1 if axis == axis_at else 1 for axis in range(drawn.ndim)]) for axis_at in (source, target)]
    chosen = jax.random.permutation(key, shards_of)[partner]
    strong = (owner == chosen) | (owner == (partner + shards_of // 2) % shards_of)
    return jnp.where(strong, factor * drawn, drawn)


def level_of(key, extent, cuts, least, top_value):
    def one(position, blocks):
        steps = jax.random.uniform(jax.random.fold_in(jax.random.fold_in(key, 6), position), (blocks,), jnp.float32, least / len(cuts), top_value / len(cuts))
        return jnp.repeat(jnp.exp(steps), extent[position] // blocks).reshape((-1,) + (1,) * (len(extent) - position - 1))

    level = one(*cuts[0])
    for cut in cuts[1:]:
        level = level * one(*cut)
    return level


def bell_draw(stream_key, shape, scale, limit, pieces=(), dtype=jnp.bfloat16):
    values = scale * jax.random.normal(stream_key, shape, jnp.float32)
    if pieces:
        values = values * level_of(stream_key, shape, pieces, -0.22, 0.18)
    return jnp.clip(values, -limit, limit).astype(dtype)


def heavy_noise(stream_key, extent, scale, bound, cuts, heavy, dtype=jnp.bfloat16):
    array = scale * jax.random.normal(stream_key, extent, jnp.float32)
    if cuts:
        array = array * level_of(stream_key, extent, cuts, -0.22, 0.18)
    return jnp.clip(strengthened(array, jax.random.fold_in(stream_key, 3), *heavy), -bound, bound).astype(dtype)


def setup_inputs(seed: int = 0) -> dict:
    key_list = jax.random.split(jax.random.key(seed), 6)
    return {
        "projected": bell_draw(key_list[0], (L, 3, C), 1.0, 6.0, ((0, 32), (2, 8))),
        "short_taps": bell_draw(key_list[1], (TAPS, 3, C), 0.4, 2.5, ((2, 8),), jnp.float32),
        "long_filter": bell_draw(key_list[2], (L, C), L ** -0.5, 0.0625, ((0, 32), (1, 8))),
        "skip_gain": jnp.clip(0.5 + 1.0 * jax.random.uniform(key_list[3], (C,), jnp.float32) ** level_of(key_list[3], (C,), ((0, 8),), -0.2, 0.2), 0.5, 1.5),
        "out_weight": heavy_noise(key_list[4], (C, C), C ** -0.5, 0.125, ((0, 8),), (0, 1, 8, 2.0)),
    }


def long_conv(gated, long_filter):
    length, channels = gated.shape
    block = min(channels, 256)
    groups = channels // block
    gated_blocks = gated.astype(jnp.float32).T.reshape(groups, block, length)
    filter_blocks = long_filter.astype(jnp.float32).T.reshape(groups, block, length)

    def one_block(pair):
        gated_part, filter_part = pair
        spectrum = jnp.fft.rfft(gated_part, n=2 * length, axis=1) * jnp.fft.rfft(filter_part, n=2 * length, axis=1)
        return jnp.fft.irfft(spectrum, n=2 * length, axis=1)[:, :length]

    result = lax.map(one_block, (gated_blocks, filter_blocks))
    return result.reshape(channels, length).T


def reference(projected, short_taps, long_filter, skip_gain, out_weight):
    rows = projected.shape[0]
    count = short_taps.shape[0]
    padded = jnp.concatenate([jnp.zeros((count - 1,) + projected.shape[1:], jnp.float32), projected.astype(jnp.float32)], axis=0)
    filtered = short_taps[0] * padded[0:rows]
    for index in range(1, count):
        filtered = filtered + short_taps[index] * padded[index:index + rows]
    gated = (filtered[:, 1] * filtered[:, 2]).astype(jnp.bfloat16)
    conv = long_conv(gated, long_filter).astype(jnp.float32)
    mixed_rows = (filtered[:, 0] * (conv + skip_gain[None, :] * gated.astype(jnp.float32))).astype(jnp.bfloat16)
    result = jnp.dot(mixed_rows.astype(jnp.float32), out_weight.astype(jnp.float32), preferred_element_type=jnp.float32)
    return result.T.astype(jnp.bfloat16)
```

```python
import functools

import jax
import jax.numpy as jnp
import ml_dtypes
import numpy as np
from jax import lax
from jax.sharding import PartitionSpec as P


def tables(blocks, width, group):
    total = 2 * blocks * width
    half = np.arange(blocks + 1)
    block = np.arange(blocks)
    inner = np.arange(width)
    eye = np.eye(group)
    outer = 2.0 * np.pi * ((half[:, None] * block[None, :]) % (2 * blocks)) / (2 * blocks)
    first = np.concatenate([np.kron(np.cos(outer), eye), np.kron(-np.sin(outer), eye)], axis=0)
    weight = np.where((half == 0) | (half == blocks), 1.0, 2.0)[:, None] / total
    last = np.concatenate(
        [np.kron((weight * np.cos(outer)).T, eye), np.kron((-weight * np.sin(outer)).T, eye)], axis=1
    )
    turn = 2.0 * np.pi * (half[:, None] * inner[None, :]) / total
    turn = np.repeat(turn, group, axis=0)
    angle = 2.0 * np.pi * ((inner[:, None] * inner[None, :]) % width) / width
    cos, sin = np.cos(angle), np.sin(angle)
    forward = np.block([[cos, -sin], [sin, cos]])
    inverse = np.block([[cos, sin], [-sin, cos]])
    narrow = lambda table: table.astype(np.float32).astype(ml_dtypes.bfloat16)
    return (
        narrow(first),
        narrow(last),
        np.cos(turn).astype(np.float32),
        np.sin(turn).astype(np.float32),
        narrow(forward),
        narrow(inverse),
    )


def product(left, right):
    return lax.dot_general(left, right, (((1,), (0,)), ((), ())), preferred_element_type=jnp.float32)


def spectrum(values, first, cos, sin, forward):
    rows = cos.shape[0]
    part = product(first, values)
    real, imag = part[:rows], part[rows:]
    turned = jnp.concatenate([real * cos + imag * sin, imag * cos - real * sin], axis=1)
    return product(turned.astype(jnp.bfloat16), forward)


def long_conv(gated, long_filter, first, last, cos, sin, forward, inverse):
    width = gated.shape[1]
    g = spectrum(gated, first, cos, sin, forward)
    h = spectrum(long_filter, first, cos, sin, forward)
    g_real, g_imag = g[:, :width], g[:, width:]
    h_real, h_imag = h[:, :width], h[:, width:]
    both = jnp.concatenate([g_real * h_real - g_imag * h_imag, g_real * h_imag + g_imag * h_real], axis=1)
    back = product(both.astype(jnp.bfloat16), inverse)
    real, imag = back[:, :width], back[:, width:]
    turned = jnp.concatenate([real * cos - imag * sin, real * sin + imag * cos], axis=0)
    return product(last, turned.astype(jnp.bfloat16))


def regroup(values, blocks):
    rows, width = values.shape
    shaped = values.reshape(blocks, rows // blocks, width)
    return lax.all_to_all(shaped, "seq", split_axis=0, concat_axis=0, tiled=True).reshape(rows, width)


def body(projected, short_taps, long_filter, skip_gain, out_weight):
    blocks = lax.axis_size("seq")
    rows, _, channels = projected.shape
    count = short_taps.shape[0]
    filter_parts = regroup(long_filter.T, blocks)
    tail = projected[rows - (count - 1) :]
    previous = lax.ppermute(tail, "seq", [(s, s + 1) for s in range(blocks - 1)])
    extended = jnp.concatenate([previous, projected], axis=0).astype(jnp.float32)
    filtered = short_taps[0] * extended[0:rows]
    for index in range(1, count):
        filtered = filtered + short_taps[index] * extended[index : index + rows]
    gated = (filtered[:, 1] * filtered[:, 2]).astype(jnp.bfloat16).T
    consts = tables(blocks, rows, channels // blocks)
    conv = long_conv(regroup(gated, blocks), filter_parts, *consts)
    conv = regroup(conv.astype(jnp.bfloat16), blocks).astype(jnp.float32)
    mixed = filtered[:, 0].T * (conv + skip_gain[:, None] * gated.astype(jnp.float32))
    partial = lax.dot_general(
        out_weight, mixed.astype(jnp.bfloat16), (((0,), (0,)), ((), ())), preferred_element_type=jnp.float32
    )
    return lax.psum_scatter(partial.astype(jnp.bfloat16), "chan", scatter_dimension=0, tiled=True)


def solution(mesh):
    in_specs = (
        P("seq", None, "chan"),
        P(None, None, "chan"),
        P("seq", "chan"),
        P("chan"),
        P("chan", None),
    )
    return jax.shard_map(body, mesh=mesh, in_specs=in_specs, out_specs=P("chan", "seq"), check_vma=False)
```

```python
import functools

import jax
import jax.numpy as jnp
import ml_dtypes
import numpy as np
from jax import lax
from jax.experimental import pallas as pl
from jax.experimental.pallas import tpu as pltpu
from jax.sharding import PartitionSpec as P

MESH = pl.DeviceIdType.MESH
PARTS = 2
LANES = 128
HALO = 16
TILES = 3


def tables(blocks, width, group):
    total = 2 * blocks * width
    half = np.arange(blocks + 1)
    block = np.arange(blocks)
    inner = np.arange(width)
    eye = np.eye(group)
    outer = 2.0 * np.pi * ((half[:, None] * block[None, :]) % (2 * blocks)) / (2 * blocks)
    first = np.concatenate([np.kron(np.cos(outer), eye), np.kron(-np.sin(outer), eye)], axis=0)
    weight = np.where((half == 0) | (half == blocks), 1.0, 2.0)[:, None] / total
    last = np.concatenate(
        [np.kron((weight * np.cos(outer)).T, eye), np.kron((-weight * np.sin(outer)).T, eye)], axis=1
    )
    turn = 2.0 * np.pi * (half[:, None] * inner[None, :]) / total
    turn = np.repeat(turn, group, axis=0)
    angle = 2.0 * np.pi * ((inner[:, None] * inner[None, :]) % width) / width
    cos, sin = np.cos(angle), np.sin(angle)
    forward = np.block([[cos, -sin], [sin, cos]])
    inverse = np.block([[cos, sin], [-sin, cos]])
    narrow = lambda table: table.astype(np.float32).astype(ml_dtypes.bfloat16)
    return (
        narrow(first),
        narrow(last),
        np.cos(turn).astype(np.float32),
        np.sin(turn).astype(np.float32),
        narrow(forward),
        narrow(inverse),
    )


def product(left, right):
    return lax.dot_general(left, right, (((1,), (0,)), ((), ())), preferred_element_type=jnp.float32)


def flipped(values):
    return values.astype(jnp.float32).T.astype(values.dtype)


def kernel(
    blocks,
    proj_hbm, taps, filt_hbm, skip, weight_hbm,
    first_hbm, last_hbm, cos_hbm, sin_hbm, forward_hbm, inverse_hbm,
    out,
    proj, halo, ext, filt, gat, f0, f_turned, f_parts, g_turned, g_parts, f0_turned, base,
    weight, w_turned, first, last, cos, sin, forward, inverse,
    h_spec, spun, y_turned, y_parts, mixed,
    pair_out, pair_in, far_out, relay_in, kept, near_out, near_in,
    load_sem, halo_sem, f_sem, g_sem, y_sem, pair_send, pair_recv, ring_send, ring_recv,
):
    parts, channels, width = y_turned.shape
    tokens = parts * width
    group = channels // blocks
    rows = cos.shape[0]
    count = taps.shape[1]
    ob = out.shape[0]
    hb = ob // 2

    me = lax.axis_index("seq")
    chan = lax.axis_index("chan")
    y_at, core = lax.div(chan, 2), lax.rem(chan, 2)
    xs = min(4, blocks)
    zs = blocks // xs
    z_me, x_me = lax.div(me, xs), lax.rem(me, xs)

    def peer(k):
        j = lax.rem(k * 13, blocks)
        z = lax.rem(z_me + lax.div(j, xs), zs)
        x = lax.rem(x_me + lax.rem(j, xs), xs)
        return z * xs + x

    def chan_of(step, core_of):
        return 2 * lax.rem(y_at + step, 4) + core_of

    sibling = chan_of(0, 1 - core)
    up, down = chan_of(1, core), chan_of(3, core)

    loads = [
        pltpu.make_async_copy(source, target, load_sem.at[index])
        for index, (source, target) in enumerate(
            [
                (filt_hbm, filt), (proj_hbm, proj), (weight_hbm, weight), (first_hbm, first),
                (cos_hbm, cos), (sin_hbm, sin), (forward_hbm, forward), (inverse_hbm, inverse),
                (last_hbm, last),
            ]
        )
    ]
    for load in loads:
        load.start()

    barrier = pltpu.get_barrier_semaphore()

    def greet(k, carry):
        pl.semaphore_signal(barrier, inc=1, device_id={"seq": peer(k)}, device_id_type=MESH)
        return carry

    lax.fori_loop(1, blocks, greet, 0)
    for other in (sibling, up, down):
        pl.semaphore_signal(barrier, inc=1, device_id={"chan": other}, device_id_type=MESH)

    def spot(index):
        return pl.ds(pl.multiple_of(index * group, group), group)

    def lane(index):
        return pl.ds(pl.multiple_of(index * LANES, LANES), LANES)

    def scatter(source, target, sems):
        def step(k, carry):
            to = peer(k)
            pltpu.make_async_remote_copy(
                src_ref=source.at[spot(to)],
                dst_ref=target.at[spot(me)],
                send_sem=sems.at[0],
                recv_sem=sems.at[1],
                device_id={"seq": to},
                device_id_type=MESH,
            ).start()
            return carry

        lax.fori_loop(1, blocks, step, 0)
        target[spot(me), :] = source[spot(me), :]

    def finish(buffer, sem):
        rest = buffer.at[pl.ds(0, (blocks - 1) * group)]
        pltpu.make_async_copy(rest, rest, sem).wait()

    loads[0].wait()

    def turn_filter(c, carry):
        f_turned[lane(c), :] = flipped(filt[:, lane(c)])
        return carry

    lax.fori_loop(0, channels // LANES, turn_filter, 0)
    loads[1].wait()
    pl.semaphore_wait(barrier, blocks - 1 + 3)

    to_next = pltpu.make_async_remote_copy(
        src_ref=proj.at[:, pl.ds(tokens - HALO, HALO), :],
        dst_ref=halo,
        send_sem=halo_sem.at[0],
        recv_sem=halo_sem.at[1],
        device_id={"seq": lax.rem(me + 1, blocks)},
        device_id_type=MESH,
    )
    to_next.start()
    scatter(f_turned, f_parts, f_sem)

    def widen(c, carry):
        for b in range(3):
            ext[b, pl.ds(8, tokens), lane(c)] = proj[b, :, lane(c)].astype(jnp.float32)
        return carry

    lax.fori_loop(0, channels // LANES, widen, 0)

    def short(c, start, size):
        def branch(b):
            total = None
            for j in range(count):
                term = taps[b, pl.ds(j, 1), lane(c)] * ext[b, pl.ds(start + 9 - count + j, size), lane(c)]
                total = term if total is None else total + term
            return total

        f0[pl.ds(start, size), lane(c)] = branch(0)
        gat[pl.ds(start, size), lane(c)] = branch(1) * branch(2)

    def short_rest(c, carry):
        short(c, 8, 56)
        for start in range(64, tokens, 64):
            short(c, start, 64)
        return carry

    lax.fori_loop(0, channels // LANES, short_rest, 0)
    to_next.wait_recv()
    live = jnp.where(me > 0, 1.0, 0.0).astype(jnp.float32)

    def short_first(c, carry):
        for b in range(3):
            ext[b, pl.ds(0, 8), lane(c)] = live * halo[b, :, lane(c)].astype(jnp.float32)[HALO - 8 :]
        short(c, 0, 8)
        g_turned[lane(c), :] = gat[:, lane(c)].T.astype(jnp.bfloat16)
        return carry

    lax.fori_loop(0, channels // LANES, short_first, 0)
    scatter(g_turned, g_parts, g_sem)

    def turn_rest(c, carry):
        turned = f0[:, lane(c)].T
        f0_turned[lane(c), :] = turned
        gain = jnp.broadcast_to(skip[:, lane(c)], (LANES, LANES)).T
        gains = jnp.concatenate([gain] * (tokens // LANES), axis=1)
        base[lane(c), :] = turned * (gains * g_turned[lane(c), :].astype(jnp.float32))
        return carry

    lax.fori_loop(0, channels // LANES, turn_rest, 0)
    loads[2].wait()

    def turn_weight(c, carry):
        w_turned[lane(c), :] = flipped(weight[:, lane(c)])
        return carry

    lax.fori_loop(0, weight.shape[1] // LANES, turn_weight, 0)
    for load in loads[3:]:
        load.wait()

    tile = rows // TILES

    def tile_of(index, shift=0):
        return pl.ds(pl.multiple_of(shift + index * tile, 16), tile)

    def spectrum(index, values):
        real = product(first[tile_of(index), :], values[...])
        imag = product(first[tile_of(index, rows), :], values[...])
        c, s = cos[tile_of(index), :], sin[tile_of(index), :]
        turned = jnp.concatenate([real * c + imag * s, imag * c - real * s], axis=1)
        return product(turned.astype(jnp.bfloat16), forward[...])

    finish(f_parts, f_sem.at[1])

    def filter_tile(index, carry):
        h_spec[tile_of(index), :] = spectrum(index, f_parts)
        return carry

    lax.fori_loop(0, TILES, filter_tile, 0)
    finish(g_parts, g_sem.at[1])

    def conv_tile(index, carry):
        g = spectrum(index, g_parts)
        h = h_spec[tile_of(index), :]
        gr, gi, hr, hi = g[:, :tokens], g[:, tokens:], h[:, :tokens], h[:, tokens:]
        both = jnp.concatenate([gr * hr - gi * hi, gr * hi + gi * hr], axis=1)
        back = product(both.astype(jnp.bfloat16), inverse[...])
        real, imag = back[:, :tokens], back[:, tokens:]
        c, s = cos[tile_of(index), :], sin[tile_of(index), :]
        spun[tile_of(index), :] = (real * c - imag * s).astype(jnp.bfloat16)
        spun[tile_of(index, rows), :] = (real * s + imag * c).astype(jnp.bfloat16)
        return carry

    lax.fori_loop(0, TILES, conv_tile, 0)

    for q in range(parts):
        columns = spun[:, q * width : (q + 1) * width]
        y_turned[q] = product(last[...], columns).astype(jnp.bfloat16)
        scatter(y_turned.at[q], y_parts.at[q], y_sem.at[q])

    def block(q, index):
        at = pl.ds(pl.multiple_of(index * ob, ob), ob)
        return product(w_turned[at, :], mixed[q])

    def pair_copy(q, k):
        return pltpu.make_async_remote_copy(
            src_ref=pair_out.at[q, k],
            dst_ref=pair_in.at[q, k],
            send_sem=pair_send.at[q, k],
            recv_sem=pair_recv.at[q, k],
            device_id={"chan": sibling},
            device_id_type=MESH,
        )

    def step_of(k):
        if isinstance(k, int):
            return (2, 1, 3, 0)[k]
        return lax.rem(2 + 3 * k + 3 * lax.div(k, 2) + 2 * lax.div(k, 3), 4)

    def ring_copy(q, index, source, target, to):
        return pltpu.make_async_remote_copy(
            src_ref=source,
            dst_ref=target,
            send_sem=ring_send.at[q, index],
            recv_sem=ring_recv.at[q, index],
            device_id={"chan": to},
            device_id_type=MESH,
        )

    def ring(q, index):
        to = down if index % 2 else up
        if index < 2:
            rows_of = pl.ds(index * hb, hb)
            return ring_copy(q, index, far_out.at[q, rows_of], relay_in.at[q, index], to)
        side = index % 2
        rows_of = pl.ds(hb if index in (2, 5) else 0, hb)
        return ring_copy(q, index, near_out.at[q, side, rows_of], near_in.at[q, side, rows_of], to)

    def stage_a(q):
        finish(y_parts.at[q], y_sem.at[q, 1])
        at = pl.ds(q * width, width)
        mixed[q] = (f0_turned[:, at] * y_parts[q].astype(jnp.float32) + base[:, at]).astype(jnp.bfloat16)

        def send(k, carry):
            pair_out[q, k] = block(q, chan_of(step_of(k), 1 - core)).astype(jnp.bfloat16)
            pair_copy(q, k).start()
            return carry

        lax.fori_loop(0, 4, send, 0)

    def chip_sum(q, k):
        mine = block(q, chan_of(step_of(k), core))
        pair_copy(q, k).wait_recv()
        return mine + pair_in[q, k].astype(jnp.float32)

    def stage_b(q):
        far_out[q] = chip_sum(q, 0).astype(jnp.bfloat16)
        ring(q, 0).start()
        ring(q, 1).start()
        above = chip_sum(q, 1)
        near_out[q, 0, pl.ds(hb, hb), :] = above[hb:].astype(jnp.bfloat16)
        ring(q, 2).start()
        kept[q, 0] = above[:hb]
        below = chip_sum(q, 2)
        near_out[q, 1, pl.ds(0, hb), :] = below[:hb].astype(jnp.bfloat16)
        ring(q, 3).start()
        kept[q, 1] = below[hb:]

    def stage_c(q):
        ring(q, 0).wait_recv()
        near_out[q, 0, pl.ds(0, hb), :] = (kept[q, 0] + relay_in[q, 0].astype(jnp.float32)).astype(jnp.bfloat16)
        ring(q, 4).start()
        ring(q, 1).wait_recv()
        near_out[q, 1, pl.ds(hb, hb), :] = (kept[q, 1] + relay_in[q, 1].astype(jnp.float32)).astype(jnp.bfloat16)
        ring(q, 5).start()

    def stage_d(q):
        own = chip_sum(q, 3)
        for index in range(2, 6):
            ring(q, index).wait_recv()
        total = own + near_in[q, 0].astype(jnp.float32) + near_in[q, 1].astype(jnp.float32)
        out[:, q * width : (q + 1) * width] = total.astype(jnp.bfloat16)

    for q in range(parts):
        stage_a(q)
        stage_b(q)
    for q in range(parts):
        stage_c(q)
    for q in range(parts):
        stage_d(q)

    to_next.wait_send()
    finish(f_turned, f_sem.at[0])
    finish(g_turned, g_sem.at[0])
    for q in range(parts):
        finish(y_turned.at[q], y_sem.at[q, 0])

        def drained(k, carry):
            pair_copy(q, k).wait_send()
            return carry

        lax.fori_loop(0, 4, drained, 0)
        for index in range(6):
            ring(q, index).wait_send()


def body(projected, short_taps, long_filter, skip_gain, out_weight):
    blocks = lax.axis_size("seq")
    tokens, branches, channels = projected.shape
    count = short_taps.shape[0]
    outs = out_weight.shape[1]
    ob = outs // lax.axis_size("chan")
    group = channels // blocks
    rows = (blocks + 1) * group
    width = tokens // PARTS
    consts = tables(blocks, tokens, group)
    bf16, f32 = jnp.bfloat16, jnp.float32
    dma = pltpu.SemaphoreType.DMA
    vmem = pl.BlockSpec(memory_space=pltpu.VMEM)
    hbm = pl.BlockSpec(memory_space=pl.ANY)
    return pl.pallas_call(
        functools.partial(kernel, blocks),
        out_shape=jax.ShapeDtypeStruct((ob, tokens), bf16),
        in_specs=[hbm, vmem, hbm, vmem, hbm] + [hbm] * 6,
        out_specs=vmem,
        scratch_shapes=[
            pltpu.VMEM((branches, tokens, channels), bf16),
            pltpu.VMEM((branches, HALO, channels), bf16),
            pltpu.VMEM((branches, tokens + 8, channels), f32),
            pltpu.VMEM((tokens, channels), bf16),
            pltpu.VMEM((tokens, channels), f32),
            pltpu.VMEM((tokens, channels), f32),
            pltpu.VMEM((channels, tokens), bf16),
            pltpu.VMEM((channels, tokens), bf16),
            pltpu.VMEM((channels, tokens), bf16),
            pltpu.VMEM((channels, tokens), bf16),
            pltpu.VMEM((channels, tokens), f32),
            pltpu.VMEM((channels, tokens), f32),
            pltpu.VMEM((channels, outs), bf16),
            pltpu.VMEM((outs, channels), bf16),
            pltpu.VMEM((2 * rows, channels), bf16),
            pltpu.VMEM((channels, 2 * rows), bf16),
            pltpu.VMEM((rows, tokens), f32),
            pltpu.VMEM((rows, tokens), f32),
            pltpu.VMEM((2 * tokens, 2 * tokens), bf16),
            pltpu.VMEM((2 * tokens, 2 * tokens), bf16),
            pltpu.VMEM((rows, 2 * tokens), f32),
            pltpu.VMEM((2 * rows, tokens), bf16),
            pltpu.VMEM((PARTS, channels, width), bf16),
            pltpu.VMEM((PARTS, channels, width), bf16),
            pltpu.VMEM((PARTS, channels, width), bf16),
            pltpu.VMEM((PARTS, 4, ob, width), bf16),
            pltpu.VMEM((PARTS, 4, ob, width), bf16),
            pltpu.VMEM((PARTS, ob, width), bf16),
            pltpu.VMEM((PARTS, 2, ob // 2, width), bf16),
            pltpu.VMEM((PARTS, 2, ob // 2, width), f32),
            pltpu.VMEM((PARTS, 2, ob, width), bf16),
            pltpu.VMEM((PARTS, 2, ob, width), bf16),
            dma((9,)),
            dma((2,)),
            dma((2,)),
            dma((2,)),
            dma((PARTS, 2)),
            dma((PARTS, 4)),
            dma((PARTS, 4)),
            dma((PARTS, 6)),
            dma((PARTS, 6)),
        ],
        compiler_params=pltpu.CompilerParams(
            collective_id=0, has_side_effects=True, vmem_limit_bytes=52 * 1024 * 1024
        ),
    )(
        jnp.transpose(projected, (1, 0, 2)),
        jnp.transpose(short_taps, (1, 0, 2)),
        long_filter,
        skip_gain.reshape(1, channels),
        out_weight,
        *[jnp.asarray(const) for const in consts],
    )


def solution(mesh):
    in_specs = (
        P("seq", None, "chan"),
        P(None, None, "chan"),
        P("seq", "chan"),
        P("chan"),
        P("chan", None),
    )
    return jax.shard_map(body, mesh=mesh, in_specs=in_specs, out_specs=P("chan", "seq"), check_vma=False)
```

```python
import functools

import jax
import jax.numpy as jnp
import ml_dtypes
import numpy as np
from jax import lax
from jax.experimental import pallas as pl
from jax.experimental.pallas import tpu as pltpu
from jax.sharding import PartitionSpec as P

MESH = pl.DeviceIdType.MESH
PARTS = 2
LANES = 128
HALO = 16
TILES = 3


def tables(blocks, width, group):
    total = 2 * blocks * width
    half = np.arange(blocks + 1)
    block = np.arange(blocks)
    inner = np.arange(width)
    eye = np.eye(group)
    outer = 2.0 * np.pi * ((half[:, None] * block[None, :]) % (2 * blocks)) / (2 * blocks)
    first = np.concatenate([np.kron(np.cos(outer), eye), np.kron(-np.sin(outer), eye)], axis=0)
    weight = np.where((half == 0) | (half == blocks), 1.0, 2.0)[:, None] / total
    last = np.concatenate(
        [np.kron((weight * np.cos(outer)).T, eye), np.kron((-weight * np.sin(outer)).T, eye)], axis=1
    )
    turn = 2.0 * np.pi * (half[:, None] * inner[None, :]) / total
    turn = np.repeat(turn, group, axis=0)
    angle = 2.0 * np.pi * ((inner[:, None] * inner[None, :]) % width) / width
    cos, sin = np.cos(angle), np.sin(angle)
    forward = np.block([[cos, -sin], [sin, cos]])
    step = width // PARTS
    inverse = np.concatenate(
        [
            np.block([[cos[:, at : at + step], sin[:, at : at + step]], [-sin[:, at : at + step], cos[:, at : at + step]]])
            for at in range(0, width, step)
        ],
        axis=1,
    )
    narrow = lambda table: table.astype(np.float32).astype(ml_dtypes.bfloat16)
    return (
        narrow(first),
        narrow(last),
        np.cos(turn).astype(np.float32),
        np.sin(turn).astype(np.float32),
        narrow(forward),
        narrow(inverse),
    )


def product(left, right):
    return lax.dot_general(left, right, (((1,), (0,)), ((), ())), preferred_element_type=jnp.float32)


def flipped(values):
    return values.astype(jnp.float32).T.astype(values.dtype)


def kernel(
    blocks,
    proj_hbm, taps_hbm, filt_hbm, skip_hbm, weight_hbm,
    first_hbm, last_hbm, cos_hbm, sin_hbm, forward_hbm, inverse_hbm,
    out,
    proj, taps, skip, halo, ext, filt, gat, f0, f_turned, f_parts, g_turned, g_parts, f0_turned, base,
    weight, w_out, w_own, w_other, first, last, cos, sin, forward, inverse,
    h_spec, both, spun, y_turned, y_parts, mixed, mixed_other, partial,
    far_out, relay_in, kept, near_out, near_in,
    load_sem, halo_sem, f_sem, g_sem, y_sem, w_send, w_recv, mix_send, mix_recv, ring_send, ring_recv,
):
    parts, channels, width = y_turned.shape
    tokens = parts * width
    group = channels // blocks
    rows = cos.shape[0]
    count = taps.shape[1]
    ob = out.shape[0]
    hb = ob // 2

    me = lax.axis_index("seq")
    chan = lax.axis_index("chan")
    y_at, core = lax.div(chan, 2), lax.rem(chan, 2)

    def peer(k):
        return jnp.where(k - 1 < me, k - 1, k)

    def chan_of(step, core_of):
        return 2 * lax.rem(y_at + step, 4) + core_of

    sibling = chan_of(0, 1 - core)
    up, down = chan_of(1, core), chan_of(3, core)

    loads = [
        pltpu.make_async_copy(source, target, load_sem.at[index])
        for index, (source, target) in enumerate(
            [
                (filt_hbm, filt), (proj_hbm, proj), (taps_hbm, taps), (skip_hbm, skip), (weight_hbm, weight), (first_hbm, first),
                (cos_hbm, cos), (sin_hbm, sin), (forward_hbm, forward), (inverse_hbm, inverse),
                (last_hbm, last),
            ]
        )
    ]
    for load in loads:
        load.start()

    barrier = pltpu.get_barrier_semaphore()

    def greet(k, carry):
        pl.semaphore_signal(barrier, inc=1, device_id={"seq": peer(k)}, device_id_type=MESH)
        return carry

    lax.fori_loop(1, blocks, greet, 0)
    for other in (sibling, up, down):
        pl.semaphore_signal(barrier, inc=1, device_id={"chan": other}, device_id_type=MESH)

    def spot(index):
        return pl.ds(pl.multiple_of(index * group, group), group)

    def lane(index):
        return pl.ds(pl.multiple_of(index * LANES, LANES), LANES)

    def scatter(source, target, sems):
        def step(k, carry):
            to = peer(k)
            pltpu.make_async_remote_copy(
                src_ref=source.at[spot(to)],
                dst_ref=target.at[spot(me)],
                send_sem=sems.at[0],
                recv_sem=sems.at[1],
                device_id={"seq": to},
                device_id_type=MESH,
            ).start()
            return carry

        lax.fori_loop(1, blocks, step, 0)
        target[spot(me), :] = source[spot(me), :]

    def finish(buffer, sem):
        rest = buffer.at[pl.ds(0, (blocks - 1) * group)]
        pltpu.make_async_copy(rest, rest, sem).wait()

    loads[0].wait()

    def turn_filter(c, carry):
        f_turned[lane(c), :] = flipped(filt[:, lane(c)])
        return carry

    lax.fori_loop(0, channels // LANES, turn_filter, 0)
    for load in loads[1:4]:
        load.wait()
    pl.semaphore_wait(barrier, blocks - 1 + 3)

    to_next = pltpu.make_async_remote_copy(
        src_ref=proj.at[:, pl.ds(tokens - HALO, HALO), :],
        dst_ref=halo,
        send_sem=halo_sem.at[0],
        recv_sem=halo_sem.at[1],
        device_id={"seq": lax.rem(me + 1, blocks)},
        device_id_type=MESH,
    )
    to_next.start()
    scatter(f_turned, f_parts, f_sem)

    def widen(c, carry):
        for b in range(3):
            ext[b, pl.ds(8, tokens), lane(c)] = proj[b, :, lane(c)].astype(jnp.float32)
        return carry

    lax.fori_loop(0, channels // LANES, widen, 0)

    def short(c, start, size):
        def branch(b):
            total = None
            for j in range(count):
                term = taps[b, pl.ds(j, 1), lane(c)] * ext[b, pl.ds(start + 9 - count + j, size), lane(c)]
                total = term if total is None else total + term
            return total

        f0[pl.ds(start, size), lane(c)] = branch(0)
        gat[pl.ds(start, size), lane(c)] = branch(1) * branch(2)

    def short_rest(c, carry):
        short(c, 8, 56)
        for start in range(64, tokens, 64):
            short(c, start, 64)
        return carry

    lax.fori_loop(0, channels // LANES, short_rest, 0)
    to_next.wait_recv()
    live = jnp.where(me > 0, 1.0, 0.0).astype(jnp.float32)

    def short_first(c, carry):
        for b in range(3):
            ext[b, pl.ds(0, 8), lane(c)] = live * halo[b, :, lane(c)].astype(jnp.float32)[HALO - 8 :]
        short(c, 0, 8)
        g_turned[lane(c), :] = gat[:, lane(c)].T.astype(jnp.bfloat16)
        return carry

    lax.fori_loop(0, channels // LANES, short_first, 0)
    scatter(g_turned, g_parts, g_sem)

    def turn_rest(c, carry):
        turned = f0[:, lane(c)].T
        f0_turned[lane(c), :] = turned
        gain = jnp.broadcast_to(skip[:, lane(c)], (LANES, LANES)).T
        gains = jnp.concatenate([gain] * (tokens // LANES), axis=1)
        base[lane(c), :] = turned * (gains * g_turned[lane(c), :].astype(jnp.float32))
        return carry

    lax.fori_loop(0, channels // LANES, turn_rest, 0)
    loads[4].wait()

    def weight_copy(j):
        return pltpu.make_async_remote_copy(
            src_ref=w_out.at[j],
            dst_ref=w_other.at[j],
            send_sem=w_send.at[j],
            recv_sem=w_recv.at[j],
            device_id={"chan": sibling},
            device_id_type=MESH,
        )

    def turn_block(target, j, core_of):
        def turn(c, carry):
            at = (2 * j + core_of) * (ob // LANES) + c
            target[j, lane(c), :] = flipped(weight[:, lane(at)])
            return carry

        lax.fori_loop(0, ob // LANES, turn, 0)

    def turn_out(j, carry):
        turn_block(w_out, j, 1 - core)
        weight_copy(j).start()
        return carry

    def turn_own(j, carry):
        turn_block(w_own, j, core)
        return carry

    lax.fori_loop(0, 4, turn_out, 0)
    lax.fori_loop(0, 4, turn_own, 0)
    for load in loads[5:]:
        load.wait()

    tile = rows // TILES

    def tile_of(index, shift=0):
        return pl.ds(pl.multiple_of(shift + index * tile, 16), tile)

    def spectrum(index, values):
        real = product(first[tile_of(index), :], values[...])
        imag = product(first[tile_of(index, rows), :], values[...])
        c, s = cos[tile_of(index), :], sin[tile_of(index), :]
        turned = jnp.concatenate([real * c + imag * s, imag * c - real * s], axis=1)
        return product(turned.astype(jnp.bfloat16), forward[...])

    finish(f_parts, f_sem.at[1])

    def filter_tile(index, carry):
        h_spec[tile_of(index), :] = spectrum(index, f_parts)
        return carry

    lax.fori_loop(0, TILES, filter_tile, 0)
    finish(g_parts, g_sem.at[1])

    def conv_tile(index, carry):
        g = spectrum(index, g_parts)
        h = h_spec[tile_of(index), :]
        gr, gi, hr, hi = g[:, :tokens], g[:, tokens:], h[:, :tokens], h[:, tokens:]
        multiplied = jnp.concatenate([gr * hr - gi * hi, gr * hi + gi * hr], axis=1).astype(jnp.bfloat16)
        both[tile_of(index), :] = multiplied
        back_tile(0, index, multiplied)
        return carry

    def back_tile(q, index, multiplied):
        back = product(multiplied, inverse[:, 2 * q * width : 2 * (q + 1) * width])
        real, imag = back[:, :width], back[:, width:]
        at = slice(q * width, (q + 1) * width)
        c, s = cos[tile_of(index), at], sin[tile_of(index), at]
        spun[q, tile_of(index), :] = (real * c - imag * s).astype(jnp.bfloat16)
        spun[q, tile_of(index, rows), :] = (real * s + imag * c).astype(jnp.bfloat16)

    lax.fori_loop(0, TILES, conv_tile, 0)

    for q in range(parts):
        if q > 0:

            def later_tile(index, carry):
                back_tile(q, index, both[tile_of(index), :])
                return carry

            lax.fori_loop(0, TILES, later_tile, 0)
        y_turned[q] = product(last[...], spun[q]).astype(jnp.bfloat16)
        scatter(y_turned.at[q], y_parts.at[q], y_sem.at[q])

    def mix_copy(q):
        return pltpu.make_async_remote_copy(
            src_ref=mixed.at[q],
            dst_ref=mixed_other.at[q],
            send_sem=mix_send.at[q],
            recv_sem=mix_recv.at[q],
            device_id={"chan": sibling},
            device_id_type=MESH,
        )

    def arrived_weight(j, carry):
        weight_copy(j).wait_recv()
        return carry

    lax.fori_loop(0, 4, arrived_weight, 0)

    def step_of(k):
        if isinstance(k, int):
            return (2, 1, 3, 0)[k]
        return lax.rem(2 + 3 * k + 3 * lax.div(k, 2) + 2 * lax.div(k, 3), 4)

    def ring_copy(q, index, source, target, to):
        return pltpu.make_async_remote_copy(
            src_ref=source,
            dst_ref=target,
            send_sem=ring_send.at[q, index],
            recv_sem=ring_recv.at[q, index],
            device_id={"chan": to},
            device_id_type=MESH,
        )

    def ring(q, index):
        to = down if index % 2 else up
        if index < 2:
            rows_of = pl.ds(index * hb, hb)
            return ring_copy(q, index, far_out.at[q, rows_of], relay_in.at[q, index], to)
        side = index % 2
        rows_of = pl.ds(hb if index in (2, 5) else 0, hb)
        return ring_copy(q, index, near_out.at[q, side, rows_of], near_in.at[q, side, rows_of], to)

    def stage_a(q):
        finish(y_parts.at[q], y_sem.at[q, 1])
        at = pl.ds(q * width, width)
        mixed[q] = (f0_turned[:, at] * y_parts[q].astype(jnp.float32) + base[:, at]).astype(jnp.bfloat16)

        mix_copy(q).start()

        def own_share(k, carry):
            partial[q, k] = product(w_own[lax.rem(y_at + step_of(k), 4)], mixed[q])
            return carry

        lax.fori_loop(0, 4, own_share, 0)
        mix_copy(q).wait_recv()

    def chip_sum(q, k):
        return partial[q, k] + product(w_other[lax.rem(y_at + step_of(k), 4)], mixed_other[q])

    def stage_b(q):
        far_out[q] = chip_sum(q, 0).astype(jnp.bfloat16)
        ring(q, 0).start()
        ring(q, 1).start()
        above = chip_sum(q, 1)
        near_out[q, 0, pl.ds(hb, hb), :] = above[hb:].astype(jnp.bfloat16)
        ring(q, 2).start()
        kept[q, 0] = above[:hb]
        below = chip_sum(q, 2)
        near_out[q, 1, pl.ds(0, hb), :] = below[:hb].astype(jnp.bfloat16)
        ring(q, 3).start()
        kept[q, 1] = below[hb:]

    def stage_c(q):
        ring(q, 0).wait_recv()
        near_out[q, 0, pl.ds(0, hb), :] = (kept[q, 0] + relay_in[q, 0].astype(jnp.float32)).astype(jnp.bfloat16)
        ring(q, 4).start()
        ring(q, 1).wait_recv()
        near_out[q, 1, pl.ds(hb, hb), :] = (kept[q, 1] + relay_in[q, 1].astype(jnp.float32)).astype(jnp.bfloat16)
        ring(q, 5).start()

    def stage_d(q):
        own = chip_sum(q, 3)
        for index in range(2, 6):
            ring(q, index).wait_recv()
        total = own + near_in[q, 0].astype(jnp.float32) + near_in[q, 1].astype(jnp.float32)
        out[:, q * width : (q + 1) * width] = total.astype(jnp.bfloat16)

    for q in range(parts):
        stage_a(q)
        stage_b(q)
    for q in range(parts):
        stage_c(q)
    for q in range(parts):
        stage_d(q)

    to_next.wait_send()

    def left_weight(j, carry):
        weight_copy(j).wait_send()
        return carry

    lax.fori_loop(0, 4, left_weight, 0)
    finish(f_turned, f_sem.at[0])
    finish(g_turned, g_sem.at[0])
    for q in range(parts):
        finish(y_turned.at[q], y_sem.at[q, 0])
        mix_copy(q).wait_send()
        for index in range(6):
            ring(q, index).wait_send()


def body(projected, short_taps, long_filter, skip_gain, out_weight):
    blocks = lax.axis_size("seq")
    tokens, branches, channels = projected.shape
    count = short_taps.shape[0]
    outs = out_weight.shape[1]
    ob = outs // lax.axis_size("chan")
    group = channels // blocks
    rows = (blocks + 1) * group
    width = tokens // PARTS
    consts = tables(blocks, tokens, group)
    bf16, f32 = jnp.bfloat16, jnp.float32
    dma = pltpu.SemaphoreType.DMA
    vmem = pl.BlockSpec(memory_space=pltpu.VMEM)
    hbm = pl.BlockSpec(memory_space=pltpu.HBM)
    return pl.pallas_call(
        functools.partial(kernel, blocks),
        out_shape=jax.ShapeDtypeStruct((ob, tokens), bf16),
        in_specs=[hbm] * 11,
        out_specs=vmem,
        scratch_shapes=[
            pltpu.VMEM((branches, tokens, channels), bf16),
            pltpu.VMEM((branches, count, channels), f32),
            pltpu.VMEM((1, channels), f32),
            pltpu.VMEM((branches, HALO, channels), bf16),
            pltpu.VMEM((branches, tokens + 8, channels), f32),
            pltpu.VMEM((tokens, channels), bf16),
            pltpu.VMEM((tokens, channels), f32),
            pltpu.VMEM((tokens, channels), f32),
            pltpu.VMEM((channels, tokens), bf16),
            pltpu.VMEM((channels, tokens), bf16),
            pltpu.VMEM((channels, tokens), bf16),
            pltpu.VMEM((channels, tokens), bf16),
            pltpu.VMEM((channels, tokens), f32),
            pltpu.VMEM((channels, tokens), f32),
            pltpu.VMEM((channels, outs), bf16),
            pltpu.VMEM((4, ob, channels), bf16),
            pltpu.VMEM((4, ob, channels), bf16),
            pltpu.VMEM((4, ob, channels), bf16),
            pltpu.VMEM((2 * rows, channels), bf16),
            pltpu.VMEM((channels, 2 * rows), bf16),
            pltpu.VMEM((rows, tokens), f32),
            pltpu.VMEM((rows, tokens), f32),
            pltpu.VMEM((2 * tokens, 2 * tokens), bf16),
            pltpu.VMEM((2 * tokens, 2 * tokens), bf16),
            pltpu.VMEM((rows, 2 * tokens), f32),
            pltpu.VMEM((rows, 2 * tokens), bf16),
            pltpu.VMEM((PARTS, 2 * rows, width), bf16),
            pltpu.VMEM((PARTS, channels, width), bf16),
            pltpu.VMEM((PARTS, channels, width), bf16),
            pltpu.VMEM((PARTS, channels, width), bf16),
            pltpu.VMEM((PARTS, channels, width), bf16),
            pltpu.VMEM((PARTS, 4, ob, width), f32),
            pltpu.VMEM((PARTS, ob, width), bf16),
            pltpu.VMEM((PARTS, 2, ob // 2, width), bf16),
            pltpu.VMEM((PARTS, 2, ob // 2, width), f32),
            pltpu.VMEM((PARTS, 2, ob, width), bf16),
            pltpu.VMEM((PARTS, 2, ob, width), bf16),
            dma((11,)),
            dma((2,)),
            dma((2,)),
            dma((2,)),
            dma((PARTS, 2)),
            dma((4,)),
            dma((4,)),
            dma((PARTS,)),
            dma((PARTS,)),
            dma((PARTS, 6)),
            dma((PARTS, 6)),
        ],
        compiler_params=pltpu.CompilerParams(
            collective_id=0, has_side_effects=True, vmem_limit_bytes=60 * 1024 * 1024
        ),
    )(
        jnp.transpose(projected, (1, 0, 2)),
        jnp.transpose(short_taps, (1, 0, 2)),
        long_filter,
        skip_gain.reshape(1, channels),
        out_weight,
        *[jnp.asarray(const) for const in consts],
    )


def solution(mesh):
    in_specs = (
        P("seq", None, "chan"),
        P(None, None, "chan"),
        P("seq", "chan"),
        P("chan"),
        P("chan", None),
    )
    return jax.shard_map(body, mesh=mesh, in_specs=in_specs, out_specs=P("chan", "seq"), check_vma=False)
```

```python
import functools

import jax
import jax.numpy as jnp
import ml_dtypes
import numpy as np
from jax import lax
from jax.experimental import pallas as pl
from jax.experimental.pallas import tpu as pltpu
from jax.sharding import PartitionSpec as P

MESH = pl.DeviceIdType.MESH
PARTS = 2
LANES = 128
HALO = 16
TILES = 1


def tables(blocks, width, group):
    total = 2 * blocks * width
    half = np.arange(blocks + 1)
    block = np.arange(blocks)
    inner = np.arange(width)
    eye = np.eye(group)
    outer = 2.0 * np.pi * ((half[:, None] * block[None, :]) % (2 * blocks)) / (2 * blocks)
    first = np.concatenate([np.kron(np.cos(outer), eye), np.kron(-np.sin(outer), eye)], axis=0)
    weight = np.where((half == 0) | (half == blocks), 1.0, 2.0)[:, None] / total
    last = np.concatenate(
        [np.kron((weight * np.cos(outer)).T, eye), np.kron((-weight * np.sin(outer)).T, eye)], axis=1
    )
    turn = 2.0 * np.pi * (half[:, None] * inner[None, :]) / total
    turn = np.repeat(turn, group, axis=0)
    angle = 2.0 * np.pi * ((inner[:, None] * inner[None, :]) % width) / width
    cos, sin = np.cos(angle), np.sin(angle)
    forward = np.block([[cos, -sin], [sin, cos]])
    step = width // PARTS
    inverse = np.concatenate(
        [
            np.block([[cos[:, at : at + step], sin[:, at : at + step]], [-sin[:, at : at + step], cos[:, at : at + step]]])
            for at in range(0, width, step)
        ],
        axis=1,
    )
    narrow = lambda table: table.astype(np.float32).astype(ml_dtypes.bfloat16)
    return (
        narrow(first),
        narrow(last),
        np.cos(turn).astype(np.float32),
        np.sin(turn).astype(np.float32),
        narrow(forward),
        narrow(inverse),
    )


def product(left, right):
    return lax.dot_general(left, right, (((1,), (0,)), ((), ())), preferred_element_type=jnp.float32)


def flipped(values):
    return values.astype(jnp.float32).T.astype(values.dtype)


def kernel(
    blocks,
    proj_hbm, taps_hbm, filt_hbm, skip_hbm, weight_hbm,
    first_hbm, last_hbm, cos_hbm, sin_hbm, forward_hbm, inverse_hbm,
    out,
    proj, taps, skip, halo, ext, filt, gat, f0, f_turned, f_parts, g_turned, g_parts, f0_turned, base,
    weight, w_out, w_own, w_other, first, last, cos, sin, forward, inverse,
    h_spec, both, spun, y_turned, y_parts, mixed, mixed_other, partial,
    far_out, relay_in, kept, near_out, near_in,
    load_sem, halo_sem, f_sem, g_sem, y_sem, w_send, w_recv, mix_send, mix_recv, ring_send, ring_recv,
):
    parts, channels, width = y_turned.shape
    tokens = parts * width
    group = channels // blocks
    rows = cos.shape[0]
    count = taps.shape[1]
    ob = out.shape[0]
    hb = ob // 2

    me = lax.axis_index("seq")
    chan = lax.axis_index("chan")
    y_at, core = lax.div(chan, 2), lax.rem(chan, 2)

    def peer(k):
        return jnp.where(k - 1 < me, k - 1, k)

    xs = min(4, blocks)
    zs = blocks // xs

    def far_first(k):
        order = lax.rem(k - 1, zs)
        near = lax.div(order + 1, 2)
        ahead = zs // 2 + jnp.where(lax.rem(order, 2) == 0, near, zs - near)
        z = lax.rem(lax.div(me, xs) + ahead, zs)
        x = lax.rem(lax.rem(me, xs) + xs - 1 - lax.div(k - 1, zs), xs)
        return z * xs + x

    def chan_of(step, core_of):
        return 2 * lax.rem(y_at + step, 4) + core_of

    sibling = chan_of(0, 1 - core)
    up, down = chan_of(1, core), chan_of(3, core)

    loads = [
        pltpu.make_async_copy(source, target, load_sem.at[index])
        for index, (source, target) in enumerate(
            [
                (filt_hbm, filt), (proj_hbm, proj), (taps_hbm, taps), (skip_hbm, skip), (weight_hbm, weight), (first_hbm, first),
                (cos_hbm, cos), (sin_hbm, sin), (forward_hbm, forward), (inverse_hbm, inverse),
                (last_hbm, last),
            ]
        )
    ]
    loads[0].start()

    barrier = pltpu.get_barrier_semaphore()

    def greet(k, carry):
        pl.semaphore_signal(barrier, inc=1, device_id={"seq": peer(k)}, device_id_type=MESH)
        return carry

    lax.fori_loop(1, blocks, greet, 0)
    for other in (sibling, up, down):
        pl.semaphore_signal(barrier, inc=1, device_id={"chan": other}, device_id_type=MESH)
    for load in loads[1:]:
        load.start()

    def spot(index):
        return pl.ds(pl.multiple_of(index * group, group), group)

    def lane(index):
        return pl.ds(pl.multiple_of(index * LANES, LANES), LANES)

    def scatter(source, target, sems, order=peer):
        def step(k, carry):
            to = order(k)
            pltpu.make_async_remote_copy(
                src_ref=source.at[spot(to)],
                dst_ref=target.at[spot(me)],
                send_sem=sems.at[0],
                recv_sem=sems.at[1],
                device_id={"seq": to},
                device_id_type=MESH,
            ).start()
            return carry

        lax.fori_loop(1, blocks, step, 0)
        target[spot(me), :] = source[spot(me), :]

    def finish(buffer, sem):
        rest = buffer.at[pl.ds(0, (blocks - 1) * group)]
        pltpu.make_async_copy(rest, rest, sem).wait()

    loads[0].wait()

    def turn_filter(c, carry):
        f_turned[lane(c), :] = flipped(filt[:, lane(c)])
        return carry

    lax.fori_loop(0, channels // LANES, turn_filter, 0)
    for load in loads[1:4]:
        load.wait()
    pl.semaphore_wait(barrier, blocks - 1 + 3)

    to_next = pltpu.make_async_remote_copy(
        src_ref=proj.at[:, pl.ds(tokens - HALO, HALO), :],
        dst_ref=halo,
        send_sem=halo_sem.at[0],
        recv_sem=halo_sem.at[1],
        device_id={"seq": lax.rem(me + 1, blocks)},
        device_id_type=MESH,
    )
    to_next.start()
    scatter(f_turned, f_parts, f_sem, far_first)

    def widen(c, carry):
        for b in range(3):
            ext[b, pl.ds(8, tokens), lane(c)] = proj[b, :, lane(c)].astype(jnp.float32)
        return carry

    lax.fori_loop(0, channels // LANES, widen, 0)

    def short(c, start, size):
        def branch(b):
            total = None
            for j in range(count):
                term = taps[b, pl.ds(j, 1), lane(c)] * ext[b, pl.ds(start + 9 - count + j, size), lane(c)]
                total = term if total is None else total + term
            return total

        f0[pl.ds(start, size), lane(c)] = branch(0)
        gat[pl.ds(start, size), lane(c)] = branch(1) * branch(2)

    def short_rest(c, carry):
        short(c, 8, 56)
        for start in range(64, tokens, 64):
            short(c, start, 64)
        return carry

    lax.fori_loop(0, channels // LANES, short_rest, 0)
    to_next.wait_recv()
    live = jnp.where(me > 0, 1.0, 0.0).astype(jnp.float32)

    def short_first(c, carry):
        for b in range(3):
            ext[b, pl.ds(0, 8), lane(c)] = live * halo[b, :, lane(c)].astype(jnp.float32)[HALO - 8 :]
        short(c, 0, 8)
        g_turned[lane(c), :] = gat[:, lane(c)].T.astype(jnp.bfloat16)
        return carry

    lax.fori_loop(0, channels // LANES, short_first, 0)
    scatter(g_turned, g_parts, g_sem, far_first)

    def turn_rest(c, carry):
        turned = f0[:, lane(c)].T
        f0_turned[lane(c), :] = turned
        gain = jnp.broadcast_to(skip[:, lane(c)], (LANES, LANES)).T
        gains = jnp.concatenate([gain] * (tokens // LANES), axis=1)
        base[lane(c), :] = turned * (gains * g_turned[lane(c), :].astype(jnp.float32))
        return carry

    lax.fori_loop(0, channels // LANES, turn_rest, 0)
    loads[4].wait()

    def weight_copy(j):
        return pltpu.make_async_remote_copy(
            src_ref=w_out.at[j],
            dst_ref=w_other.at[j],
            send_sem=w_send.at[j],
            recv_sem=w_recv.at[j],
            device_id={"chan": sibling},
            device_id_type=MESH,
        )

    def turn_block(target, j, core_of):
        def turn(c, carry):
            at = (2 * j + core_of) * (ob // LANES) + c
            target[j, lane(c), :] = flipped(weight[:, lane(at)])
            return carry

        lax.fori_loop(0, ob // LANES, turn, 0)

    def turn_out(j, carry):
        turn_block(w_out, j, 1 - core)
        weight_copy(j).start()
        return carry

    def turn_own(j, carry):
        turn_block(w_own, j, core)
        return carry

    lax.fori_loop(0, 4, turn_out, 0)
    lax.fori_loop(0, 4, turn_own, 0)
    for load in loads[5:]:
        load.wait()

    tile = rows // TILES

    def tile_of(index, shift=0):
        return pl.ds(pl.multiple_of(shift + index * tile, 16), tile)

    def spectrum(index, values):
        real = product(first[tile_of(index), :], values[...])
        imag = product(first[tile_of(index, rows), :], values[...])
        c, s = cos[tile_of(index), :], sin[tile_of(index), :]
        turned = jnp.concatenate([real * c + imag * s, imag * c - real * s], axis=1)
        return product(turned.astype(jnp.bfloat16), forward[...])

    finish(f_parts, f_sem.at[1])

    def filter_tile(index, carry):
        h_spec[tile_of(index), :] = spectrum(index, f_parts)
        return carry

    lax.fori_loop(0, TILES, filter_tile, 0)
    finish(g_parts, g_sem.at[1])

    def conv_tile(index, carry):
        g = spectrum(index, g_parts)
        h = h_spec[tile_of(index), :]
        gr, gi, hr, hi = g[:, :tokens], g[:, tokens:], h[:, :tokens], h[:, tokens:]
        multiplied = jnp.concatenate([gr * hr - gi * hi, gr * hi + gi * hr], axis=1).astype(jnp.bfloat16)
        both[tile_of(index), :] = multiplied
        back_tile(0, index, multiplied)
        return carry

    def back_tile(q, index, multiplied):
        back = product(multiplied, inverse[:, 2 * q * width : 2 * (q + 1) * width])
        real, imag = back[:, :width], back[:, width:]
        at = slice(q * width, (q + 1) * width)
        c, s = cos[tile_of(index), at], sin[tile_of(index), at]
        spun[q, tile_of(index), :] = (real * c - imag * s).astype(jnp.bfloat16)
        spun[q, tile_of(index, rows), :] = (real * s + imag * c).astype(jnp.bfloat16)

    lax.fori_loop(0, TILES, conv_tile, 0)

    for q in range(parts):
        if q > 0:

            def later_tile(index, carry):
                back_tile(q, index, both[tile_of(index), :])
                return carry

            lax.fori_loop(0, TILES, later_tile, 0)
        y_turned[q] = product(last[...], spun[q]).astype(jnp.bfloat16)
        scatter(y_turned.at[q], y_parts.at[q], y_sem.at[q])

    def mix_copy(q):
        return pltpu.make_async_remote_copy(
            src_ref=mixed.at[q],
            dst_ref=mixed_other.at[q],
            send_sem=mix_send.at[q],
            recv_sem=mix_recv.at[q],
            device_id={"chan": sibling},
            device_id_type=MESH,
        )

    def arrived_weight(j, carry):
        weight_copy(j).wait_recv()
        return carry

    lax.fori_loop(0, 4, arrived_weight, 0)

    def step_of(k):
        if isinstance(k, int):
            return (2, 1, 3, 0)[k]
        return lax.rem(2 + 3 * k + 3 * lax.div(k, 2) + 2 * lax.div(k, 3), 4)

    def ring_copy(q, index, source, target, to):
        return pltpu.make_async_remote_copy(
            src_ref=source,
            dst_ref=target,
            send_sem=ring_send.at[q, index],
            recv_sem=ring_recv.at[q, index],
            device_id={"chan": to},
            device_id_type=MESH,
        )

    def ring(q, index):
        to = down if index % 2 else up
        if index < 2:
            rows_of = pl.ds(index * hb, hb)
            return ring_copy(q, index, far_out.at[q, rows_of], relay_in.at[q, index], to)
        side = index % 2
        rows_of = pl.ds(hb if index in (2, 5) else 0, hb)
        return ring_copy(q, index, near_out.at[q, side, rows_of], near_in.at[q, side, rows_of], to)

    def stage_a(q):
        finish(y_parts.at[q], y_sem.at[q, 1])
        at = pl.ds(q * width, width)
        mixed[q] = (f0_turned[:, at] * y_parts[q].astype(jnp.float32) + base[:, at]).astype(jnp.bfloat16)

        mix_copy(q).start()

        def own_share(k, carry):
            partial[q, k] = product(w_own[lax.rem(y_at + step_of(k), 4)], mixed[q])
            return carry

        lax.fori_loop(0, 4, own_share, 0)
        mix_copy(q).wait_recv()

    def chip_sum(q, k):
        return partial[q, k] + product(w_other[lax.rem(y_at + step_of(k), 4)], mixed_other[q])

    def stage_b(q):
        far_out[q] = chip_sum(q, 0).astype(jnp.bfloat16)
        ring(q, 0).start()
        ring(q, 1).start()
        above = chip_sum(q, 1)
        near_out[q, 0, pl.ds(hb, hb), :] = above[hb:].astype(jnp.bfloat16)
        ring(q, 2).start()
        kept[q, 0] = above[:hb]
        below = chip_sum(q, 2)
        near_out[q, 1, pl.ds(0, hb), :] = below[:hb].astype(jnp.bfloat16)
        ring(q, 3).start()
        kept[q, 1] = below[hb:]

    def stage_c(q):
        ring(q, 0).wait_recv()
        near_out[q, 0, pl.ds(0, hb), :] = (kept[q, 0] + relay_in[q, 0].astype(jnp.float32)).astype(jnp.bfloat16)
        ring(q, 4).start()
        ring(q, 1).wait_recv()
        near_out[q, 1, pl.ds(hb, hb), :] = (kept[q, 1] + relay_in[q, 1].astype(jnp.float32)).astype(jnp.bfloat16)
        ring(q, 5).start()

    def stage_d(q):
        own = chip_sum(q, 3)
        for index in range(2, 6):
            ring(q, index).wait_recv()
        total = own + near_in[q, 0].astype(jnp.float32) + near_in[q, 1].astype(jnp.float32)
        out[:, q * width : (q + 1) * width] = total.astype(jnp.bfloat16)

    for q in range(parts):
        stage_a(q)
        stage_b(q)
    for q in range(parts):
        stage_c(q)
    for q in range(parts):
        stage_d(q)

    to_next.wait_send()

    def left_weight(j, carry):
        weight_copy(j).wait_send()
        return carry

    lax.fori_loop(0, 4, left_weight, 0)
    finish(f_turned, f_sem.at[0])
    finish(g_turned, g_sem.at[0])
    for q in range(parts):
        finish(y_turned.at[q], y_sem.at[q, 0])
        mix_copy(q).wait_send()
        for index in range(6):
            ring(q, index).wait_send()


def body(projected, short_taps, long_filter, skip_gain, out_weight):
    blocks = lax.axis_size("seq")
    tokens, branches, channels = projected.shape
    count = short_taps.shape[0]
    outs = out_weight.shape[1]
    ob = outs // lax.axis_size("chan")
    group = channels // blocks
    rows = (blocks + 1) * group
    width = tokens // PARTS
    consts = tables(blocks, tokens, group)
    bf16, f32 = jnp.bfloat16, jnp.float32
    dma = pltpu.SemaphoreType.DMA
    vmem = pl.BlockSpec(memory_space=pltpu.VMEM)
    hbm = pl.BlockSpec(memory_space=pltpu.HBM)
    return pl.pallas_call(
        functools.partial(kernel, blocks),
        out_shape=jax.ShapeDtypeStruct((ob, tokens), bf16),
        in_specs=[hbm] * 11,
        out_specs=vmem,
        scratch_shapes=[
            pltpu.VMEM((branches, tokens, channels), bf16),
            pltpu.VMEM((branches, count, channels), f32),
            pltpu.VMEM((1, channels), f32),
            pltpu.VMEM((branches, HALO, channels), bf16),
            pltpu.VMEM((branches, tokens + 8, channels), f32),
            pltpu.VMEM((tokens, channels), bf16),
            pltpu.VMEM((tokens, channels), f32),
            pltpu.VMEM((tokens, channels), f32),
            pltpu.VMEM((channels, tokens), bf16),
            pltpu.VMEM((channels, tokens), bf16),
            pltpu.VMEM((channels, tokens), bf16),
            pltpu.VMEM((channels, tokens), bf16),
            pltpu.VMEM((channels, tokens), f32),
            pltpu.VMEM((channels, tokens), f32),
            pltpu.VMEM((channels, outs), bf16),
            pltpu.VMEM((4, ob, channels), bf16),
            pltpu.VMEM((4, ob, channels), bf16),
            pltpu.VMEM((4, ob, channels), bf16),
            pltpu.VMEM((2 * rows, channels), bf16),
            pltpu.VMEM((channels, 2 * rows), bf16),
            pltpu.VMEM((rows, tokens), f32),
            pltpu.VMEM((rows, tokens), f32),
            pltpu.VMEM((2 * tokens, 2 * tokens), bf16),
            pltpu.VMEM((2 * tokens, 2 * tokens), bf16),
            pltpu.VMEM((rows, 2 * tokens), f32),
            pltpu.VMEM((rows, 2 * tokens), bf16),
            pltpu.VMEM((PARTS, 2 * rows, width), bf16),
            pltpu.VMEM((PARTS, channels, width), bf16),
            pltpu.VMEM((PARTS, channels, width), bf16),
            pltpu.VMEM((PARTS, channels, width), bf16),
            pltpu.VMEM((PARTS, channels, width), bf16),
            pltpu.VMEM((PARTS, 4, ob, width), f32),
            pltpu.VMEM((PARTS, ob, width), bf16),
            pltpu.VMEM((PARTS, 2, ob // 2, width), bf16),
            pltpu.VMEM((PARTS, 2, ob // 2, width), f32),
            pltpu.VMEM((PARTS, 2, ob, width), bf16),
            pltpu.VMEM((PARTS, 2, ob, width), bf16),
            dma((11,)),
            dma((2,)),
            dma((2,)),
            dma((2,)),
            dma((PARTS, 2)),
            dma((4,)),
            dma((4,)),
            dma((PARTS,)),
            dma((PARTS,)),
            dma((PARTS, 6)),
            dma((PARTS, 6)),
        ],
        compiler_params=pltpu.CompilerParams(
            collective_id=0, has_side_effects=True, vmem_limit_bytes=60 * 1024 * 1024
        ),
    )(
        jnp.transpose(projected, (1, 0, 2)),
        jnp.transpose(short_taps, (1, 0, 2)),
        long_filter,
        skip_gain.reshape(1, channels),
        out_weight,
        *[jnp.asarray(const) for const in consts],
    )


def solution(mesh):
    in_specs = (
        P("seq", None, "chan"),
        P(None, None, "chan"),
        P("seq", "chan"),
        P("chan"),
        P("chan", None),
    )
    return jax.shard_map(body, mesh=mesh, in_specs=in_specs, out_specs=P("chan", "seq"), check_vma=False)
```

```python
import functools

import jax
import jax.numpy as jnp
import ml_dtypes
import numpy as np
from jax import lax
from jax.experimental import pallas as pl
from jax.experimental.pallas import tpu as pltpu
from jax.sharding import PartitionSpec as P

MESH = pl.DeviceIdType.MESH
PARTS = 2
LANES = 128
HALO = 16
TILES = 1


def tables(blocks, width, group):
    total = 2 * blocks * width
    half = np.arange(blocks + 1)
    block = np.arange(blocks)
    inner = np.arange(width)
    eye = np.eye(group)
    outer = 2.0 * np.pi * ((half[:, None] * block[None, :]) % (2 * blocks)) / (2 * blocks)
    first = np.concatenate([np.kron(np.cos(outer), eye), np.kron(-np.sin(outer), eye)], axis=0)
    weight = np.where((half == 0) | (half == blocks), 1.0, 2.0)[:, None] / total
    last = np.concatenate(
        [np.kron((weight * np.cos(outer)).T, eye), np.kron((-weight * np.sin(outer)).T, eye)], axis=1
    )
    turn = 2.0 * np.pi * (half[:, None] * inner[None, :]) / total
    turn = np.repeat(turn, group, axis=0)
    angle = 2.0 * np.pi * ((inner[:, None] * inner[None, :]) % width) / width
    cos, sin = np.cos(angle), np.sin(angle)
    forward = np.block([[cos, -sin], [sin, cos]])
    step = width // PARTS
    inverse = np.concatenate(
        [
            np.block([[cos[:, at : at + step], sin[:, at : at + step]], [-sin[:, at : at + step], cos[:, at : at + step]]])
            for at in range(0, width, step)
        ],
        axis=1,
    )
    narrow = lambda table: table.astype(np.float32).astype(ml_dtypes.bfloat16)
    return (
        narrow(first),
        narrow(last),
        np.cos(turn).astype(np.float32),
        np.sin(turn).astype(np.float32),
        narrow(forward),
        narrow(inverse),
    )


def product(left, right):
    return lax.dot_general(left, right, (((1,), (0,)), ((), ())), preferred_element_type=jnp.float32)


def flipped(values):
    return values.T


def kernel(
    blocks,
    proj_hbm, taps_hbm, filt_hbm, skip_hbm, weight_hbm,
    first_hbm, last_hbm, cos_hbm, sin_hbm, forward_hbm, inverse_hbm,
    out,
    proj, taps, skip, halo, ext, filt, gat, f0, f_turned, f_parts, g_turned, g_parts, f0_turned, base,
    weight, w_out, w_own, w_other, first, last, cos, sin, forward, inverse,
    h_spec, both, spun, y_turned, y_parts, mixed, mixed_other, partial,
    far_out, relay_in, kept, near_out, near_in,
    load_sem, halo_sem, f_sem, g_sem, y_sem, w_send, w_recv, mix_send, mix_recv, ring_send, ring_recv,
):
    parts, channels, width = y_turned.shape
    tokens = parts * width
    group = channels // blocks
    rows = cos.shape[0]
    count = taps.shape[1]
    ob = out.shape[0]
    hb = ob // 2

    me = lax.axis_index("seq")
    chan = lax.axis_index("chan")
    y_at, core = lax.div(chan, 2), lax.rem(chan, 2)

    def peer(k):
        return jnp.where(k - 1 < me, k - 1, k)

    xs = min(4, blocks)
    zs = blocks // xs

    def far_first(k):
        order = lax.rem(k - 1, zs)
        near = lax.div(order + 1, 2)
        ahead = zs // 2 + jnp.where(lax.rem(order, 2) == 0, near, zs - near)
        z = lax.rem(lax.div(me, xs) + ahead, zs)
        x = lax.rem(lax.rem(me, xs) + xs - 1 - lax.div(k - 1, zs), xs)
        return z * xs + x

    def chan_of(step, core_of):
        return 2 * lax.rem(y_at + step, 4) + core_of

    sibling = chan_of(0, 1 - core)
    up, down = chan_of(1, core), chan_of(3, core)

    loads = [
        pltpu.make_async_copy(source, target, load_sem.at[index])
        for index, (source, target) in enumerate(
            [
                (filt_hbm, filt), (proj_hbm, proj), (taps_hbm, taps), (skip_hbm, skip), (weight_hbm, weight), (first_hbm, first),
                (cos_hbm, cos), (sin_hbm, sin), (forward_hbm, forward), (inverse_hbm, inverse),
                (last_hbm, last),
            ]
        )
    ]
    loads[0].start()

    barrier = pltpu.get_barrier_semaphore()

    def greet(k, carry):
        pl.semaphore_signal(barrier, inc=1, device_id={"seq": peer(k)}, device_id_type=MESH)
        return carry

    lax.fori_loop(1, blocks, greet, 0, unroll=True)
    for other in (sibling, up, down):
        pl.semaphore_signal(barrier, inc=1, device_id={"chan": other}, device_id_type=MESH)
    for load in loads[1:]:
        load.start()

    def spot(index):
        return pl.ds(pl.multiple_of(index * group, group), group)

    def lane(index):
        return pl.ds(pl.multiple_of(index * LANES, LANES), LANES)

    def scatter(source, target, sems, order=peer):
        def step(k, carry):
            to = order(k)
            pltpu.make_async_remote_copy(
                src_ref=source.at[spot(to)],
                dst_ref=target.at[spot(me)],
                send_sem=sems.at[0],
                recv_sem=sems.at[1],
                device_id={"seq": to},
                device_id_type=MESH,
            ).start()
            return carry

        lax.fori_loop(1, blocks, step, 0, unroll=True)
        target[spot(me), :] = source[spot(me), :]

    def finish(buffer, sem):
        rest = buffer.at[pl.ds(0, (blocks - 1) * group)]
        pltpu.make_async_copy(rest, rest, sem).wait()

    loads[0].wait()

    def turn_filter(c, carry):
        f_turned[lane(c), :] = flipped(filt[:, lane(c)])
        return carry

    lax.fori_loop(0, channels // LANES, turn_filter, 0)
    for load in loads[1:4]:
        load.wait()
    pl.semaphore_wait(barrier, blocks - 1 + 3)

    to_next = pltpu.make_async_remote_copy(
        src_ref=proj.at[:, pl.ds(tokens - HALO, HALO), :],
        dst_ref=halo,
        send_sem=halo_sem.at[0],
        recv_sem=halo_sem.at[1],
        device_id={"seq": lax.rem(me + 1, blocks)},
        device_id_type=MESH,
    )
    to_next.start()
    scatter(f_turned, f_parts, f_sem, far_first)

    def widen(c, carry):
        for b in range(3):
            ext[b, pl.ds(8, tokens), lane(c)] = proj[b, :, lane(c)].astype(jnp.float32)
        return carry

    lax.fori_loop(0, channels // LANES, widen, 0)

    def short(c, start, size):
        def branch(b):
            total = None
            for j in range(count):
                term = taps[b, pl.ds(j, 1), lane(c)] * ext[b, pl.ds(start + 9 - count + j, size), lane(c)]
                total = term if total is None else total + term
            return total

        f0[pl.ds(start, size), lane(c)] = branch(0)
        gat[pl.ds(start, size), lane(c)] = branch(1) * branch(2)

    def short_rest(c, carry):
        short(c, 8, 56)
        for start in range(64, tokens, 64):
            short(c, start, 64)
        return carry

    lax.fori_loop(0, channels // LANES, short_rest, 0)
    to_next.wait_recv()
    live = jnp.where(me > 0, 1.0, 0.0).astype(jnp.float32)

    def short_first(c, carry):
        for b in range(3):
            ext[b, pl.ds(0, 8), lane(c)] = live * halo[b, :, lane(c)].astype(jnp.float32)[HALO - 8 :]
        short(c, 0, 8)
        g_turned[lane(c), :] = gat[:, lane(c)].T.astype(jnp.bfloat16)
        return carry

    lax.fori_loop(0, channels // LANES, short_first, 0)
    scatter(g_turned, g_parts, g_sem, far_first)

    def turn_rest(c, carry):
        turned = f0[:, lane(c)].T
        f0_turned[lane(c), :] = turned
        gain = jnp.broadcast_to(skip[:, lane(c)], (LANES, LANES)).T
        gains = jnp.concatenate([gain] * (tokens // LANES), axis=1)
        base[lane(c), :] = turned * (gains * g_turned[lane(c), :].astype(jnp.float32))
        return carry

    lax.fori_loop(0, channels // LANES, turn_rest, 0)
    loads[4].wait()

    def weight_copy(j):
        return pltpu.make_async_remote_copy(
            src_ref=w_out.at[j],
            dst_ref=w_other.at[j],
            send_sem=w_send.at[j],
            recv_sem=w_recv.at[j],
            device_id={"chan": sibling},
            device_id_type=MESH,
        )

    def turn_block(target, j, core_of):
        def turn(c, carry):
            at = (2 * j + core_of) * (ob // LANES) + c
            target[j, lane(c), :] = flipped(weight[:, lane(at)])
            return carry

        lax.fori_loop(0, ob // LANES, turn, 0)

    def turn_out(j, carry):
        turn_block(w_out, j, 1 - core)
        weight_copy(j).start()
        return carry

    def turn_own(j, carry):
        turn_block(w_own, j, core)
        return carry

    lax.fori_loop(0, 4, turn_out, 0)
    lax.fori_loop(0, 4, turn_own, 0)
    for load in loads[5:]:
        load.wait()

    tile = rows // TILES

    def tile_of(index, shift=0):
        return pl.ds(pl.multiple_of(shift + index * tile, 16), tile)

    def spectrum(index, values):
        real = product(first[tile_of(index), :], values[...])
        imag = product(first[tile_of(index, rows), :], values[...])
        c, s = cos[tile_of(index), :], sin[tile_of(index), :]
        turned = jnp.concatenate([real * c + imag * s, imag * c - real * s], axis=1)
        return product(turned.astype(jnp.bfloat16), forward[...])

    finish(f_parts, f_sem.at[1])

    def filter_tile(index, carry):
        h_spec[tile_of(index), :] = spectrum(index, f_parts)
        return carry

    lax.fori_loop(0, TILES, filter_tile, 0)
    finish(g_parts, g_sem.at[1])

    def conv_tile(index, carry):
        g = spectrum(index, g_parts)
        h = h_spec[tile_of(index), :]
        gr, gi, hr, hi = g[:, :tokens], g[:, tokens:], h[:, :tokens], h[:, tokens:]
        multiplied = jnp.concatenate([gr * hr - gi * hi, gr * hi + gi * hr], axis=1).astype(jnp.bfloat16)
        both[tile_of(index), :] = multiplied
        back_tile(0, index, multiplied)
        return carry

    def back_tile(q, index, multiplied):
        back = product(multiplied, inverse[:, 2 * q * width : 2 * (q + 1) * width])
        real, imag = back[:, :width], back[:, width:]
        at = slice(q * width, (q + 1) * width)
        c, s = cos[tile_of(index), at], sin[tile_of(index), at]
        spun[q, tile_of(index), :] = (real * c - imag * s).astype(jnp.bfloat16)
        spun[q, tile_of(index, rows), :] = (real * s + imag * c).astype(jnp.bfloat16)

    lax.fori_loop(0, TILES, conv_tile, 0)

    for q in range(parts):
        if q > 0:

            def later_tile(index, carry):
                back_tile(q, index, both[tile_of(index), :])
                return carry

            lax.fori_loop(0, TILES, later_tile, 0)
        y_turned[q] = product(last[...], spun[q]).astype(jnp.bfloat16)
        scatter(y_turned.at[q], y_parts.at[q], y_sem.at[q])

    def mix_copy(q):
        return pltpu.make_async_remote_copy(
            src_ref=mixed.at[q],
            dst_ref=mixed_other.at[q],
            send_sem=mix_send.at[q],
            recv_sem=mix_recv.at[q],
            device_id={"chan": sibling},
            device_id_type=MESH,
        )

    def arrived_weight(j, carry):
        weight_copy(j).wait_recv()
        return carry

    lax.fori_loop(0, 4, arrived_weight, 0)

    def step_of(k):
        if isinstance(k, int):
            return (2, 1, 3, 0)[k]
        return lax.rem(2 + 3 * k + 3 * lax.div(k, 2) + 2 * lax.div(k, 3), 4)

    def ring_copy(q, index, source, target, to):
        return pltpu.make_async_remote_copy(
            src_ref=source,
            dst_ref=target,
            send_sem=ring_send.at[q, index],
            recv_sem=ring_recv.at[q, index],
            device_id={"chan": to},
            device_id_type=MESH,
        )

    def ring(q, index):
        to = down if index % 2 else up
        if index < 2:
            rows_of = pl.ds(index * hb, hb)
            return ring_copy(q, index, far_out.at[q, rows_of], relay_in.at[q, index], to)
        side = index % 2
        rows_of = pl.ds(hb if index in (2, 5) else 0, hb)
        return ring_copy(q, index, near_out.at[q, side, rows_of], near_in.at[q, side, rows_of], to)

    def stage_a(q):
        finish(y_parts.at[q], y_sem.at[q, 1])
        at = pl.ds(q * width, width)
        mixed[q] = (f0_turned[:, at] * y_parts[q].astype(jnp.float32) + base[:, at]).astype(jnp.bfloat16)

        mix_copy(q).start()

        def own_share(k, carry):
            partial[q, k] = product(w_own[lax.rem(y_at + step_of(k), 4)], mixed[q])
            return carry

        lax.fori_loop(0, 4, own_share, 0)
        mix_copy(q).wait_recv()

    def chip_sum(q, k):
        return partial[q, k] + product(w_other[lax.rem(y_at + step_of(k), 4)], mixed_other[q])

    def stage_far(q):
        far_out[q] = chip_sum(q, 0).astype(jnp.bfloat16)
        ring(q, 0).start()
        ring(q, 1).start()

    def stage_b(q):
        above = chip_sum(q, 1)
        near_out[q, 0, pl.ds(hb, hb), :] = above[hb:].astype(jnp.bfloat16)
        ring(q, 2).start()
        kept[q, 0] = above[:hb]
        below = chip_sum(q, 2)
        near_out[q, 1, pl.ds(0, hb), :] = below[:hb].astype(jnp.bfloat16)
        ring(q, 3).start()
        kept[q, 1] = below[hb:]

    def stage_c(q):
        ring(q, 0).wait_recv()
        near_out[q, 0, pl.ds(0, hb), :] = (kept[q, 0] + relay_in[q, 0].astype(jnp.float32)).astype(jnp.bfloat16)
        ring(q, 4).start()
        ring(q, 1).wait_recv()
        near_out[q, 1, pl.ds(hb, hb), :] = (kept[q, 1] + relay_in[q, 1].astype(jnp.float32)).astype(jnp.bfloat16)
        ring(q, 5).start()

    def stage_d(q):
        own = chip_sum(q, 3)
        for index in range(2, 6):
            ring(q, index).wait_recv()
        total = own + near_in[q, 0].astype(jnp.float32) + near_in[q, 1].astype(jnp.float32)
        out[:, q * width : (q + 1) * width] = total.astype(jnp.bfloat16)

    for q in range(parts):
        stage_a(q)
        stage_far(q)
        if q > 0:
            stage_c(q - 1)
        stage_b(q)
    stage_c(parts - 1)
    for q in range(parts):
        stage_d(q)

    to_next.wait_send()

    def left_weight(j, carry):
        weight_copy(j).wait_send()
        return carry

    lax.fori_loop(0, 4, left_weight, 0)
    finish(f_turned, f_sem.at[0])
    finish(g_turned, g_sem.at[0])
    for q in range(parts):
        finish(y_turned.at[q], y_sem.at[q, 0])
        mix_copy(q).wait_send()
        for index in range(6):
            ring(q, index).wait_send()


def body(projected, short_taps, long_filter, skip_gain, out_weight):
    blocks = lax.axis_size("seq")
    tokens, branches, channels = projected.shape
    count = short_taps.shape[0]
    outs = out_weight.shape[1]
    ob = outs // lax.axis_size("chan")
    group = channels // blocks
    rows = (blocks + 1) * group
    width = tokens // PARTS
    consts = tables(blocks, tokens, group)
    bf16, f32 = jnp.bfloat16, jnp.float32
    dma = pltpu.SemaphoreType.DMA
    vmem = pl.BlockSpec(memory_space=pltpu.VMEM)
    hbm = pl.BlockSpec(memory_space=pltpu.HBM)
    return pl.pallas_call(
        functools.partial(kernel, blocks),
        out_shape=jax.ShapeDtypeStruct((ob, tokens), bf16),
        in_specs=[hbm] * 11,
        out_specs=vmem,
        scratch_shapes=[
            pltpu.VMEM((branches, tokens, channels), bf16),
            pltpu.VMEM((branches, count, channels), f32),
            pltpu.VMEM((1, channels), f32),
            pltpu.VMEM((branches, HALO, channels), bf16),
            pltpu.VMEM((branches, tokens + 8, channels), f32),
            pltpu.VMEM((tokens, channels), bf16),
            pltpu.VMEM((tokens, channels), f32),
            pltpu.VMEM((tokens, channels), f32),
            pltpu.VMEM((channels, tokens), bf16),
            pltpu.VMEM((channels, tokens), bf16),
            pltpu.VMEM((channels, tokens), bf16),
            pltpu.VMEM((channels, tokens), bf16),
            pltpu.VMEM((channels, tokens), f32),
            pltpu.VMEM((channels, tokens), f32),
            pltpu.VMEM((channels, outs), bf16),
            pltpu.VMEM((4, ob, channels), bf16),
            pltpu.VMEM((4, ob, channels), bf16),
            pltpu.VMEM((4, ob, channels), bf16),
            pltpu.VMEM((2 * rows, channels), bf16),
            pltpu.VMEM((channels, 2 * rows), bf16),
            pltpu.VMEM((rows, tokens), f32),
            pltpu.VMEM((rows, tokens), f32),
            pltpu.VMEM((2 * tokens, 2 * tokens), bf16),
            pltpu.VMEM((2 * tokens, 2 * tokens), bf16),
            pltpu.VMEM((rows, 2 * tokens), f32),
            pltpu.VMEM((rows, 2 * tokens), bf16),
            pltpu.VMEM((PARTS, 2 * rows, width), bf16),
            pltpu.VMEM((PARTS, channels, width), bf16),
            pltpu.VMEM((PARTS, channels, width), bf16),
            pltpu.VMEM((PARTS, channels, width), bf16),
            pltpu.VMEM((PARTS, channels, width), bf16),
            pltpu.VMEM((PARTS, 4, ob, width), f32),
            pltpu.VMEM((PARTS, ob, width), bf16),
            pltpu.VMEM((PARTS, 2, ob // 2, width), bf16),
            pltpu.VMEM((PARTS, 2, ob // 2, width), f32),
            pltpu.VMEM((PARTS, 2, ob, width), bf16),
            pltpu.VMEM((PARTS, 2, ob, width), bf16),
            dma((11,)),
            dma((2,)),
            dma((2,)),
            dma((2,)),
            dma((PARTS, 2)),
            dma((4,)),
            dma((4,)),
            dma((PARTS,)),
            dma((PARTS,)),
            dma((PARTS, 6)),
            dma((PARTS, 6)),
        ],
        compiler_params=pltpu.CompilerParams(
            collective_id=0, has_side_effects=True, vmem_limit_bytes=60 * 1024 * 1024
        ),
    )(
        jnp.transpose(projected, (1, 0, 2)),
        jnp.transpose(short_taps, (1, 0, 2)),
        long_filter,
        skip_gain.reshape(1, channels),
        out_weight,
        *[jnp.asarray(const) for const in consts],
    )


def solution(mesh):
    in_specs = (
        P("seq", None, "chan"),
        P(None, None, "chan"),
        P("seq", "chan"),
        P("chan"),
        P("chan", None),
    )
    return jax.shard_map(body, mesh=mesh, in_specs=in_specs, out_specs=P("chan", "seq"), check_vma=False)
```
